32 devices in a mesh: groups: 2 (over x), expert: 8 (over z, y), tensor: 2 (over core).
Axes of the slice: x: 2, y: 2, z: 4, core: 2. Of those that a mesh axis runs over, the one named last changes fastest.
Arguments:
- stream: bfloat16 [4096, 4096], P(('groups', 'expert'), 'tensor'), parts along dimension 0, may hold values from -6 to 6
- query_heads: bfloat16 [4096, 2048], P(('groups', 'expert'), 'tensor'), parts along dimension 0, may hold values from -9 to 9
- key_heads: bfloat16 [4096, 512], P(('groups', 'expert'), 'tensor'), parts along dimension 0, may hold values from -4 to 4
- value_heads: bfloat16 [4096, 512], P(('groups', 'expert'), 'tensor'), parts along dimension 0, may hold values from -6 to 6
- out_proj: bfloat16 [2048, 4096], P('tensor', 'expert'), may hold values from -0.5 to 0.5
- down_proj: bfloat16 [4096, 1024], P('tensor', 'expert'), may hold values from -0.09375 to 0.09375
- expert_in: bfloat16 [32, 1024, 1024], P('expert', None, 'tensor'), may hold values from -0.1875 to 0.1875
- expert_out: bfloat16 [32, 1024, 1024], P('expert', 'tensor'), may hold values from -0.1875 to 0.1875
- up_proj: bfloat16 [1024, 4096], P('tensor', 'expert'), may hold values from -0.1875 to 0.1875
- expert_ids: int32 [4096, 6], P(('groups', 'expert')), parts along dimension 0, may hold values from 0 to 31, all different within a row; in each aligned block of 256 rows (0 to 255, 256 to 511, ...) at most 72 rows name the same one
- route_weights: int32 [4096, 6], P(('groups', 'expert')), parts along dimension 0, may hold values from 410 to 4095
Outputs:
- mixed: bfloat16 [4096, 4096], P(('groups', 'expert'), 'tensor'), parts along dimension 0
The draws below stay inside these ranges and needn't reach their ends.
There are 2 independent parts, one for each index of `groups`. The reference program is written for one: setup_inputs(seed, part) draws one part's arguments, and reference() takes and returns one part's arrays. A program takes and returns all parts, laid end to end along the dimension named above; an argument that names none is the same for every part. Nothing has to cross between parts.
Inputs may be any that keep to these rules, and one draw needn't show every extreme that they name: `expert_ids`: each row names 6 different experts; within the rows of one sequence no expert is named more than 72 times.
All inputs are finite; a program needn't handle non-finite values.
Results may differ from the reference program's by a relative error of at most 0.013.
Values may be sent and summed in bfloat16 or wider, within the bound.
A program may use at most 128 MiB of HBM per device.

```python
import math
import jax
import jax.numpy as jnp
import numpy as np
from jax import lax

D = 4096
HEADS = 16
KV_HEADS = 4
HD = 128
LATENT = 1024
FF_E = 1024
TOP = 6
TOK_DEV = 256
EXPERTS = 32
TOKENS = 2048
CAP = 72
N_EXPERT = 8
N_TENSOR = 2


def draw_query_heads(key, part):
    key = jax.random.fold_in(key, 1)
    drawn = jnp.clip(jax.random.normal(key, (TOKENS, HEADS * HD), jnp.float32), -4.0, 4.0)
    return drawn.astype(jnp.bfloat16)


def draw_key_heads(key, part):
    key = jax.random.fold_in(key, 2)
    drawn = jnp.clip(jax.random.normal(key, (TOKENS, KV_HEADS * HD), jnp.float32), -4.0, 4.0)
    return drawn.astype(jnp.bfloat16)


def plant(result, key, smallest, high):
    index_at = [jax.random.randint(jax.random.fold_in(key, axis), (), 0, length) for axis, length in enumerate(result.shape)]
    widest = result.shape.index(max(result.shape))
    next_to = index_at[:widest] + [(index_at[widest] + 1) % result.shape[widest]] + index_at[widest + 1:]
    return result.at[tuple(index_at)].set(smallest).at[tuple(next_to)].set(high)


def level_of(rng, extent, cuts, low, top_value):
    loudness, own = 1.0, jax.random.fold_in(rng, 6)
    for dim, blocks in cuts:
        steps = jnp.exp(jax.random.uniform(jax.random.fold_in(own, dim), (blocks,), jnp.float32, low / len(cuts), top_value / len(cuts)))
        loudness = loudness * jnp.repeat(steps, extent[dim] // blocks).reshape([-1 if axis == dim else 1 for axis in range(len(extent))])
    return loudness


def routed_block(stream_key, own, number, rows, count, top, bound, skew):
    order = jax.random.permutation(stream_key, count)
    heavy_load, ordinary = shares(count, rows * top, bound, skew, True), shares(count, rows * top, bound, skew, False)
    places = jnp.arange(count)

    def named(tallies, turn):
        used = int((tallies > 0).sum())
        fixed = max(1, used // 4)
        passed = fixed + (places - fixed + turn * (used - fixed)) % max(1, count - fixed)
        return jnp.zeros((count,), jnp.int32).at[order[jnp.where(places < fixed, places, passed)]].set(jnp.asarray(tallies, jnp.int32))

    tallies = jnp.where(number % 4 == 0, named(heavy_load, number // 4), named(ordinary, number - number // 4 - 1))
    mixed = jax.random.permutation(jax.random.fold_in(own, 3), count)
    giver, receiver = mixed[0:count // 2 * 2:2], mixed[1:count // 2 * 2:2]
    margin = jnp.minimum(tallies[giver] - 1, bound - tallies[receiver]) // 2
    margin = jnp.where((giver == order[0]) | (receiver == order[0]) | (tallies[receiver] == 0), 0, jnp.maximum(margin, 0))
    passed = jax.random.randint(jax.random.fold_in(own, 4), (count // 2,), 0, 1 << 20) % (margin + 1)
    tallies = tallies.at[giver].add(-passed).at[receiver].add(passed)
    items = jnp.searchsorted(jnp.cumsum(tallies), jnp.arange(rows * top), side="right").astype(jnp.int32)
    table = items.reshape(top, rows).T
    table = table[jax.random.permutation(jax.random.fold_in(own, 1), rows)]
    turn = jax.random.randint(jax.random.fold_in(own, 2), (rows, 1), 0, top)
    return jnp.take_along_axis(table, (jnp.arange(top)[None, :] + turn) % top, axis=1)


def shares(count, total, reach, slope, full):
    portions = [(1 << 20) // math.isqrt(grade ** slope) + 1 for grade in range(1, count + 1)]
    largest = reach if full else min(reach, max(-(-total // count), total * portions[0] // sum(portions)))
    least = 1 if total - largest >= count - 1 else 0
    counts, spare = [largest] + [least] * (count - 1), total - largest - least * (count - 1)
    while spare > 0:
        movable = [i for i in range(1, count) if counts[i] < largest] or [i for i in range(1, count) if counts[i] < reach]
        pool, budget = sum([portions[i] for i in movable]), spare
        for i in movable:
            addition = min(reach - counts[i], max(1, budget * portions[i] // pool), spare)
            counts[i] = counts[i] + addition
            spare = spare - addition
    return np.array(counts)


def normal_values(rng, extent, spread, most, shards=(), kind=jnp.bfloat16):
    entries = spread * jax.random.normal(rng, extent, jnp.float32)
    if shards:
        entries = entries * level_of(rng, extent, shards, -0.22, 0.18)
    return jnp.clip(entries, -most, most).astype(kind)


def setup_inputs(seed: int = 0, part: int = 0) -> dict:
    streams_of = jax.random.split(jax.random.key(seed), 12)
    own_keys = jax.random.split(jax.random.fold_in(streams_of[11], part), 12)
    stream = normal_values(own_keys[0], (TOKENS, D), 1.0, 6.0, ((0, 8), (1, 2)))
    query_heads = draw_query_heads(jax.random.fold_in(jax.random.fold_in(streams_of[11], part), 71), part)
    key_heads = draw_key_heads(jax.random.fold_in(jax.random.fold_in(streams_of[11], part), 71), part)
    value_heads = normal_values(own_keys[3], (TOKENS, KV_HEADS * HD), 1.0, 6.0, ((0, 8), (1, 2)))
    out_proj = normal_values(streams_of[4], (HEADS * HD, D), HD ** -0.5, 0.5, ((0, 2), (1, 8)))
    down_proj = normal_values(streams_of[5], (D, LATENT), D ** -0.5, 0.09375, ((0, 2), (1, 8)))
    expert_in = normal_values(streams_of[6], (EXPERTS, LATENT, FF_E), LATENT ** -0.5, 0.1875, ((0, 8), (2, 2)))
    expert_out = normal_values(streams_of[7], (EXPERTS, FF_E, LATENT), FF_E ** -0.5, 0.1875, ((0, 8), (1, 2)))
    up_proj = normal_values(streams_of[8], (LATENT, D), LATENT ** -0.5, 0.1875, ((0, 2), (1, 8)))
    expert_ids_keys = jax.random.split(jax.random.fold_in(own_keys[9], 1), TOKENS // TOK_DEV)
    expert_ids_turns = jax.random.permutation(jax.random.fold_in(own_keys[9], 3), TOKENS // TOK_DEV)
    expert_ids = jax.vmap(lambda own, number: routed_block(jax.random.fold_in(own_keys[9], 2), own, number, TOK_DEV, EXPERTS, TOP, CAP, 2))(expert_ids_keys, expert_ids_turns).reshape((TOKENS, TOP))
    route_weights = plant(jax.random.randint(own_keys[10], (TOKENS, TOP), 410, 4096), jax.random.fold_in(own_keys[10], 1), 410, 4095).astype(jnp.int32)
    return {"stream": stream, "query_heads": query_heads, "key_heads": key_heads, "value_heads": value_heads, "out_proj": out_proj, "down_proj": down_proj, "expert_in": expert_in, "expert_out": expert_out, "up_proj": up_proj, "expert_ids": expert_ids, "route_weights": route_weights}


def attend(query_rows, key_rows, value_rows):
    length = query_rows.shape[0]
    kv_local = key_rows.shape[1] // HD
    group_size = query_rows.shape[1] // key_rows.shape[1]
    queries = query_rows.astype(jnp.float32).reshape(length, kv_local, group_size, HD)
    keys_f = key_rows.astype(jnp.float32).reshape(length, kv_local, HD)
    values_f = value_rows.astype(jnp.float32).reshape(length, kv_local, HD)
    scores = jnp.einsum('tkgd,skd->kgts', queries, keys_f) * (1.0 / math.sqrt(HD))
    row_ids = lax.broadcasted_iota(jnp.int32, (length, length), 0)
    col_ids = lax.broadcasted_iota(jnp.int32, (length, length), 1)
    scores = jnp.where(col_ids <= row_ids, scores, -jnp.inf)
    highest = lax.optimization_barrier(jnp.max(scores, axis=-1, keepdims=True))
    exponent = jnp.exp(scores - highest)
    weights = (exponent / lax.optimization_barrier(jnp.sum(exponent, axis=-1, keepdims=True))).astype(jnp.bfloat16)
    attended = jnp.einsum('kgts,skd->tkgd', weights.astype(jnp.float32), values_f)
    return attended.reshape(length, -1).astype(jnp.bfloat16)

def run_expert(operands):
    rows_in, weight_in, weight_out = operands
    pre_act = jnp.dot(rows_in, weight_in, preferred_element_type=jnp.float32)
    squared = jnp.square(jnp.maximum(pre_act, 0.0)).astype(jnp.bfloat16)
    half_width = FF_E // N_TENSOR
    total = jnp.zeros((rows_in.shape[0], LATENT), jnp.float32)
    for part_index in range(N_TENSOR):
        lower = part_index * half_width
        piece = jnp.dot(squared[:, lower:lower + half_width], weight_out[lower:lower + half_width], preferred_element_type=jnp.float32).astype(jnp.bfloat16)
        piece = lax.optimization_barrier(piece)
        total = total + piece.astype(jnp.float32)
    return total.astype(jnp.bfloat16)

def reference(stream, query_heads, key_heads, value_heads, out_proj, down_proj, expert_in, expert_out, up_proj, expert_ids, route_weights):
    query_blocks = query_heads.reshape(N_EXPERT, TOK_DEV, -1)
    key_blocks = key_heads.reshape(N_EXPERT, TOK_DEV, -1)
    value_blocks = value_heads.reshape(N_EXPERT, TOK_DEV, -1)
    heads_out = lax.map(lambda triple: attend(triple[0], triple[1], triple[2]), (query_blocks, key_blocks, value_blocks))
    heads_out = heads_out.reshape(TOKENS, -1)
    attention = jnp.dot(heads_out, out_proj, preferred_element_type=jnp.float32)
    hidden = (stream.astype(jnp.float32) + attention).astype(jnp.bfloat16)
    latent = jnp.dot(hidden, down_proj, preferred_element_type=jnp.float32).astype(jnp.bfloat16)
    flat_ids = expert_ids.reshape(N_EXPERT, TOK_DEV * TOP)
    onehot = (flat_ids[:, :, None] == jnp.arange(EXPERTS, dtype=jnp.int32)[None, None, :]).astype(jnp.int32)
    before = jnp.cumsum(onehot, axis=1) - onehot
    slot_index = lax.optimization_barrier(jnp.sum(before * onehot, axis=2))
    block_index = jnp.arange(N_EXPERT, dtype=jnp.int32)[:, None]
    target = (flat_ids * (N_EXPERT * CAP) + block_index * CAP + slot_index).reshape(-1).astype(jnp.int32)
    source = (block_index * TOK_DEV + jnp.arange(TOK_DEV * TOP, dtype=jnp.int32)[None, :] // TOP).reshape(-1).astype(jnp.int32)
    buffer_rows = jnp.zeros((EXPERTS * N_EXPERT * CAP, LATENT), jnp.bfloat16).at[target].set(latent[source])
    buffer_rows = buffer_rows.reshape(EXPERTS, N_EXPERT * CAP, LATENT)
    results = lax.map(run_expert, (buffer_rows, expert_in, expert_out)).reshape(EXPERTS * N_EXPERT * CAP, LATENT)
    route_scale = route_weights.reshape(-1).astype(jnp.float32) / 4096.0
    picked = results[target].astype(jnp.float32) * route_scale[:, None]
    combined = lax.optimization_barrier(jnp.sum(picked.reshape(TOKENS, TOP, LATENT), axis=1)).astype(jnp.bfloat16)
    lifted = jnp.dot(combined, up_proj, preferred_element_type=jnp.float32)
    return (hidden.astype(jnp.float32) + lifted).astype(jnp.bfloat16)
```

```python
import math

import jax
import jax.numpy as jnp
from jax import lax
from jax.sharding import PartitionSpec as P

HD = 128
ROWS = 2048


def attend(query_rows, key_rows, value_rows):
    length = query_rows.shape[0]
    kv_local = key_rows.shape[1] // HD
    group_size = query_rows.shape[1] // key_rows.shape[1]
    queries = query_rows.reshape(length, kv_local, group_size, HD)
    keys_in = key_rows.reshape(length, kv_local, HD)
    values_in = value_rows.reshape(length, kv_local, HD)
    scores = jnp.einsum("tkgd,skd->kgts", queries, keys_in, preferred_element_type=jnp.float32) * (
        1.0 / math.sqrt(HD)
    )
    row_ids = lax.broadcasted_iota(jnp.int32, (length, length), 0)
    col_ids = lax.broadcasted_iota(jnp.int32, (length, length), 1)
    scores = jnp.where(col_ids <= row_ids, scores, -jnp.inf)
    highest = jnp.max(scores, axis=-1, keepdims=True)
    exponent = jnp.exp(scores - highest)
    weights = (exponent / jnp.sum(exponent, axis=-1, keepdims=True)).astype(jnp.bfloat16)
    attended = jnp.einsum("kgts,skd->tkgd", weights, values_in, preferred_element_type=jnp.float32)
    return attended.reshape(length, -1).astype(jnp.bfloat16)


def shards(
    stream,
    query_heads,
    key_heads,
    value_heads,
    out_proj,
    down_proj,
    expert_in,
    expert_out,
    up_proj,
    expert_ids,
    route_weights,
):
    length = stream.shape[0]
    heads_out = attend(query_heads, key_heads, value_heads)
    attention = jnp.dot(
        heads_out,
        lax.all_gather(out_proj, "expert", axis=1, tiled=True),
        preferred_element_type=jnp.float32,
    )
    attention = lax.psum_scatter(attention, "tensor", scatter_dimension=1, tiled=True)
    hidden = (stream.astype(jnp.float32) + attention).astype(jnp.bfloat16)
    latent_part = jnp.dot(
        hidden,
        lax.all_gather(down_proj, "expert", axis=1, tiled=True),
        preferred_element_type=jnp.float32,
    )
    rank_count = lax.axis_size("expert")
    local_experts = expert_in.shape[0]
    expert_count = local_experts * rank_count
    route_scale = route_weights.astype(jnp.float32) / 4096.0
    chosen = expert_ids[:, :, None] == jnp.arange(expert_count, dtype=jnp.int32)[None, None, :]
    gates = jnp.sum(jnp.where(chosen, route_scale[:, :, None], 0.0), axis=1)
    gates = lax.all_gather(gates, "expert", axis=0, tiled=True)
    gates = lax.dynamic_slice_in_dim(
        gates, lax.axis_index("expert") * local_experts, local_experts, axis=1
    )
    latent = lax.psum_scatter(latent_part, "tensor", scatter_dimension=0, tiled=True)
    latent = lax.all_gather(
        latent.astype(jnp.bfloat16), ("expert", "tensor"), axis=0, tiled=True
    )
    hidden_units = expert_in.shape[2]
    weight_in = expert_in.transpose(1, 0, 2).reshape(latent.shape[1], -1)
    weight_out = expert_out.reshape(-1, expert_out.shape[2])
    totals = []
    for start in range(0, latent.shape[0], ROWS):
        rows = latent[start : start + ROWS]
        pre_act = jnp.dot(rows, weight_in, preferred_element_type=jnp.float32)
        gate_rows = jnp.repeat(gates[start : start + ROWS], hidden_units, axis=1)
        squared = jnp.square(jnp.maximum(pre_act, 0.0)) * gate_rows
        totals.append(
            jnp.dot(
                squared.astype(jnp.bfloat16), weight_out, preferred_element_type=jnp.float32
            ).astype(jnp.bfloat16)
        )
    total = jnp.concatenate(totals, axis=0)
    combined = lax.psum_scatter(total, "tensor", scatter_dimension=1, tiled=True)
    combined = lax.psum_scatter(combined, "expert", scatter_dimension=0, tiled=True)
    lifted = jnp.dot(
        combined,
        lax.all_gather(up_proj, "expert", axis=1, tiled=True),
        preferred_element_type=jnp.float32,
    )
    lifted = lax.psum_scatter(lifted, "tensor", scatter_dimension=1, tiled=True)
    return (hidden.astype(jnp.float32) + lifted).astype(jnp.bfloat16)


def solution(mesh):
    return jax.shard_map(
        shards,
        mesh=mesh,
        in_specs=(
            P(("groups", "expert"), "tensor"),
            P(("groups", "expert"), "tensor"),
            P(("groups", "expert"), "tensor"),
            P(("groups", "expert"), "tensor"),
            P("tensor", "expert"),
            P("tensor", "expert"),
            P("expert", None, "tensor"),
            P("expert", "tensor", None),
            P("tensor", "expert"),
            P(("groups", "expert"), None),
            P(("groups", "expert"), None),
        ),
        out_specs=P(("groups", "expert"), "tensor"),
        check_vma=False,
    )
```

```python
import math

import jax
import jax.numpy as jnp
from jax import lax
from jax.experimental import pallas as pl
from jax.experimental.pallas import tpu as pltpu
from jax.sharding import PartitionSpec as P

HD = 128
ROWS = 2048


def attend(query_rows, key_rows, value_rows):
    length = query_rows.shape[0]
    kv_local = key_rows.shape[1] // HD
    group_size = query_rows.shape[1] // key_rows.shape[1]
    queries = query_rows.reshape(length, kv_local, group_size, HD)
    keys_in = key_rows.reshape(length, kv_local, HD)
    values_in = value_rows.reshape(length, kv_local, HD)
    scores = jnp.einsum("tkgd,skd->kgts", queries, keys_in, preferred_element_type=jnp.float32) * (
        1.0 / math.sqrt(HD)
    )
    row_ids = lax.broadcasted_iota(jnp.int32, (length, length), 0)
    col_ids = lax.broadcasted_iota(jnp.int32, (length, length), 1)
    scores = jnp.where(col_ids <= row_ids, scores, -jnp.inf)
    highest = jnp.max(scores, axis=-1, keepdims=True)
    exponent = jnp.exp(scores - highest)
    weights = (exponent / jnp.sum(exponent, axis=-1, keepdims=True)).astype(jnp.bfloat16)
    attended = jnp.einsum("kgts,skd->tkgd", weights, values_in, preferred_element_type=jnp.float32)
    return attended.reshape(length, -1).astype(jnp.bfloat16)


Z_CHIPS = 4
Y_CHIPS = 2


def gather_kernel(count, *refs):
    shard_refs, out_refs = refs[:count], refs[count : 2 * count]
    local_sem, up_sem, down_sem, y_sem, x_sem, yq_sem, xq_sem, z_in, y_in, x_in, yq_in, xq_in = refs[
        2 * count :
    ]
    group, place = lax.axis_index("groups"), lax.axis_index("expert")
    z, y = place // Y_CHIPS, place % Y_CHIPS
    up, down = {"expert": place + Y_CHIPS}, {"expert": place - Y_CHIPS}
    across, other = {"expert": z * Y_CHIPS + 1 - y}, {"groups": 1 - group}
    mesh_type = pl.DeviceIdType.MESH
    has_up, has_down = z < Z_CHIPS - 1, z > 0

    barrier = pltpu.get_barrier_semaphore()
    pl.semaphore_signal(barrier, inc=1, device_id=across, device_id_type=mesh_type)
    pl.semaphore_signal(barrier, inc=1, device_id=other, device_id_type=mesh_type)

    @pl.when(has_up)
    def _():
        pl.semaphore_signal(barrier, inc=1, device_id=up, device_id_type=mesh_type)

    @pl.when(has_down)
    def _():
        pl.semaphore_signal(barrier, inc=1, device_id=down, device_id_type=mesh_type)

    above = (2 * Z_CHIPS - 3 - z) // (Z_CHIPS - 1)
    below = (z + Z_CHIPS - 2) // (Z_CHIPS - 1)
    pl.semaphore_wait(barrier, 2 + above + below)

    def rows_of(k, half, quarter):
        half_rows = shard_refs[k].shape[0] // 2
        if quarter is None:
            return pl.ds(pl.multiple_of(half * half_rows, 16), half_rows)
        part = half_rows // 2
        return pl.ds(pl.multiple_of(half * half_rows + quarter * part, 16), part)

    def view(k, bz, by, half, quarter=None):
        wide = shard_refs[k].shape[1]
        start = pl.multiple_of((bz * Y_CHIPS + by) * wide, 128)
        return out_refs[k].at[rows_of(k, half, quarter), pl.ds(start, wide)]

    def move(k, bz, by, half, quarter, send, recv, target, own=False):
        there = view(k, bz, by, half, quarter)
        here = shard_refs[k].at[rows_of(k, half, quarter), :] if own else there
        return pltpu.make_async_remote_copy(
            src_ref=here,
            dst_ref=there,
            send_sem=send.at[k, bz],
            recv_sem=recv.at[k, bz],
            device_id=target,
            device_id_type=mesh_type,
        )

    def go_up(k, bz, own=False):
        return move(k, bz, y, group, None, up_sem, z_in, up, own)

    def go_down(k, bz, own=False):
        return move(k, bz, y, group, None, down_sem, z_in, down, own)

    def go_y(k, bz, by, own=False):
        return move(k, bz, by, group, None, y_sem, y_in, across, own)

    def go_x(k, bz, half):
        return move(k, bz, y, half, None, x_sem, x_in, other)

    def go_yq(k, bz, by, half, own=False):
        return move(k, bz, by, half, 1, yq_sem, yq_in, across, own)

    def go_xq(k, bz, half):
        return move(k, bz, 1 - y, half, 0, xq_sem, xq_in, other)

    def keep(k):
        wide = shard_refs[k].shape[1]
        start = pl.multiple_of(place * wide, 128)
        return pltpu.make_async_copy(
            shard_refs[k], out_refs[k].at[:, pl.ds(start, wide)], local_sem.at[k]
        )

    for k in range(count):

        @pl.when(has_up)
        def _(k=k):
            go_up(k, z, True).start()

        @pl.when(has_down)
        def _(k=k):
            go_down(k, z, True).start()

        go_y(k, z, y, True).start()
        go_yq(k, z, y, 1 - group, True).start()
        keep(k).start()

    for k in range(count):
        for step in range(1, Z_CHIPS):

            @pl.when(z - step >= 0)
            def _(k=k, step=step):
                block = z - step
                go_up(k, block).wait_recv()

                @pl.when(has_up)
                def _():
                    go_up(k, block).start()

                go_x(k, block, group).start()
                go_y(k, block, y).start()

            @pl.when(z + step < Z_CHIPS)
            def _(k=k, step=step):
                block = z + step
                go_down(k, block).wait_recv()

                @pl.when(has_down)
                def _():
                    go_down(k, block).start()

                go_x(k, block, group).start()
                go_y(k, block, y).start()

    for k in range(count):
        for block in range(Z_CHIPS):
            go_y(k, block, 1 - y).wait_recv()
            go_xq(k, block, group).start()

            @pl.when(z != block)
            def _(k=k, block=block):
                go_x(k, block, 1 - group).wait_recv()
                go_yq(k, block, y, 1 - group).start()

    for k in range(count):
        keep(k).wait()
        for block in range(Z_CHIPS):
            go_xq(k, block, 1 - group).wait_recv()
            go_yq(k, block, 1 - y, 1 - group).wait_recv()
            go_xq(k, block, group).wait_send()
            go_yq(k, block, y, 1 - group).wait_send()
            go_y(k, block, y).wait_send()

            @pl.when(z != block)
            def _(k=k, block=block):
                go_x(k, block, group).wait_send()

            @pl.when(jnp.logical_and(has_up, block <= z))
            def _(k=k, block=block):
                go_up(k, block).wait_send()

            @pl.when(jnp.logical_and(has_down, block >= z))
            def _(k=k, block=block):
                go_down(k, block).wait_send()


def gather_columns(*shards_in):
    count, ranks = len(shards_in), lax.axis_size("expert")
    fits = all(a.shape[1] % 128 == 0 and a.shape[0] % 64 == 0 for a in shards_in)
    if ranks != Z_CHIPS * Y_CHIPS or lax.axis_size("groups") != 2 or not fits:
        return [lax.all_gather(a, "expert", axis=1, tiled=True) for a in shards_in]
    return pl.pallas_call(
        lambda *refs: gather_kernel(count, *refs),
        out_shape=[
            jax.ShapeDtypeStruct((a.shape[0], a.shape[1] * ranks), a.dtype) for a in shards_in
        ],
        in_specs=[pl.BlockSpec(memory_space=pl.ANY)] * count,
        out_specs=[pl.BlockSpec(memory_space=pl.ANY)] * count,
        scratch_shapes=[pltpu.SemaphoreType.DMA((count,))]
        + [pltpu.SemaphoreType.DMA((count, Z_CHIPS))] * 11,
        compiler_params=pltpu.CompilerParams(collective_id=0, has_side_effects=True),
    )(*shards_in)


def shards(
    stream,
    query_heads,
    key_heads,
    value_heads,
    out_proj,
    down_proj,
    expert_in,
    expert_out,
    up_proj,
    expert_ids,
    route_weights,
):
    length = stream.shape[0]
    out_full, down_full, up_full = gather_columns(out_proj, down_proj, up_proj)
    heads_out = attend(query_heads, key_heads, value_heads)
    attention = jnp.dot(
        heads_out,
        out_full,
        preferred_element_type=jnp.float32,
    )
    attention = lax.psum_scatter(attention, "tensor", scatter_dimension=1, tiled=True)
    hidden = (stream.astype(jnp.float32) + attention).astype(jnp.bfloat16)
    latent_part = jnp.dot(
        hidden,
        down_full,
        preferred_element_type=jnp.float32,
    )
    rank_count = lax.axis_size("expert")
    local_experts = expert_in.shape[0]
    expert_count = local_experts * rank_count
    route_scale = route_weights.astype(jnp.float32) / 4096.0
    chosen = expert_ids[:, :, None] == jnp.arange(expert_count, dtype=jnp.int32)[None, None, :]
    gates = jnp.sum(jnp.where(chosen, route_scale[:, :, None], 0.0), axis=1)
    gates = lax.all_gather(gates, "expert", axis=0, tiled=True)
    gates = lax.dynamic_slice_in_dim(
        gates, lax.axis_index("expert") * local_experts, local_experts, axis=1
    )
    latent = lax.psum_scatter(latent_part, "tensor", scatter_dimension=0, tiled=True)
    latent = lax.all_gather(
        latent.astype(jnp.bfloat16), ("expert", "tensor"), axis=0, tiled=True
    )
    hidden_units = expert_in.shape[2]
    weight_in = expert_in.transpose(1, 0, 2).reshape(latent.shape[1], -1)
    weight_out = expert_out.reshape(-1, expert_out.shape[2])
    totals = []
    for start in range(0, latent.shape[0], ROWS):
        rows = latent[start : start + ROWS]
        pre_act = jnp.dot(rows, weight_in, preferred_element_type=jnp.float32)
        gate_rows = jnp.repeat(gates[start : start + ROWS], hidden_units, axis=1)
        squared = jnp.square(jnp.maximum(pre_act, 0.0)) * gate_rows
        totals.append(
            jnp.dot(
                squared.astype(jnp.bfloat16), weight_out, preferred_element_type=jnp.float32
            ).astype(jnp.bfloat16)
        )
    total = jnp.concatenate(totals, axis=0)
    combined = lax.psum_scatter(total, "tensor", scatter_dimension=1, tiled=True)
    combined = lax.psum_scatter(combined, "expert", scatter_dimension=0, tiled=True)
    lifted = jnp.dot(
        combined,
        up_full,
        preferred_element_type=jnp.float32,
    )
    lifted = lax.psum_scatter(lifted, "tensor", scatter_dimension=1, tiled=True)
    return (hidden.astype(jnp.float32) + lifted).astype(jnp.bfloat16)


def solution(mesh):
    return jax.shard_map(
        shards,
        mesh=mesh,
        in_specs=(
            P(("groups", "expert"), "tensor"),
            P(("groups", "expert"), "tensor"),
            P(("groups", "expert"), "tensor"),
            P(("groups", "expert"), "tensor"),
            P("tensor", "expert"),
            P("tensor", "expert"),
            P("expert", None, "tensor"),
            P("expert", "tensor", None),
            P("tensor", "expert"),
            P(("groups", "expert"), None),
            P(("groups", "expert"), None),
        ),
        out_specs=P(("groups", "expert"), "tensor"),
        check_vma=False,
    )
```

```python
import math

import jax
import jax.numpy as jnp
from jax import lax
from jax.experimental import pallas as pl
from jax.experimental.pallas import tpu as pltpu
from jax.sharding import PartitionSpec as P

HD = 128
ROWS = 2048


def attend(query_rows, key_rows, value_rows):
    length = query_rows.shape[0]
    kv_local = key_rows.shape[1] // HD
    group_size = query_rows.shape[1] // key_rows.shape[1]
    queries = query_rows.reshape(length, kv_local, group_size, HD)
    keys_in = key_rows.reshape(length, kv_local, HD)
    values_in = value_rows.reshape(length, kv_local, HD)
    scores = jnp.einsum("tkgd,skd->kgts", queries, keys_in, preferred_element_type=jnp.float32) * (
        1.0 / math.sqrt(HD)
    )
    row_ids = lax.broadcasted_iota(jnp.int32, (length, length), 0)
    col_ids = lax.broadcasted_iota(jnp.int32, (length, length), 1)
    scores = jnp.where(col_ids <= row_ids, scores, -jnp.inf)
    highest = jnp.max(scores, axis=-1, keepdims=True)
    exponent = jnp.exp(scores - highest)
    weights = (exponent / jnp.sum(exponent, axis=-1, keepdims=True)).astype(jnp.bfloat16)
    attended = jnp.einsum("kgts,skd->tkgd", weights, values_in, preferred_element_type=jnp.float32)
    return attended.reshape(length, -1).astype(jnp.bfloat16)


Z_CHIPS = 4
Y_CHIPS = 2


def gather_kernel(count, *refs):
    shard_refs, out_refs = refs[:count], refs[count : 2 * count]
    local_sem, up_sem, down_sem, y_sem, x_sem, yq_sem, xq_sem, z_in, y_in, x_in, yq_in, xq_in = refs[
        2 * count :
    ]
    group, place = lax.axis_index("groups"), lax.axis_index("expert")
    z, y = place // Y_CHIPS, place % Y_CHIPS
    up, down = {"expert": place + Y_CHIPS}, {"expert": place - Y_CHIPS}
    across, other = {"expert": z * Y_CHIPS + 1 - y}, {"groups": 1 - group}
    mesh_type = pl.DeviceIdType.MESH
    has_up, has_down = z < Z_CHIPS - 1, z > 0

    barrier = pltpu.get_barrier_semaphore()
    pl.semaphore_signal(barrier, inc=1, device_id=across, device_id_type=mesh_type)
    pl.semaphore_signal(barrier, inc=1, device_id=other, device_id_type=mesh_type)

    @pl.when(has_up)
    def _():
        pl.semaphore_signal(barrier, inc=1, device_id=up, device_id_type=mesh_type)

    @pl.when(has_down)
    def _():
        pl.semaphore_signal(barrier, inc=1, device_id=down, device_id_type=mesh_type)

    above = (2 * Z_CHIPS - 3 - z) // (Z_CHIPS - 1)
    below = (z + Z_CHIPS - 2) // (Z_CHIPS - 1)
    pl.semaphore_wait(barrier, 2 + above + below)

    def rows_of(k, half, quarter):
        half_rows = shard_refs[k].shape[0] // 2
        if quarter is None:
            return pl.ds(pl.multiple_of(half * half_rows, 16), half_rows)
        part = half_rows // 2
        return pl.ds(pl.multiple_of(half * half_rows + quarter * part, 16), part)

    def view(k, bz, by, half, quarter=None):
        wide = shard_refs[k].shape[1]
        start = pl.multiple_of((bz * Y_CHIPS + by) * wide, 128)
        return out_refs[k].at[rows_of(k, half, quarter), pl.ds(start, wide)]

    def move(k, bz, by, half, quarter, send, recv, target, own=False):
        there = view(k, bz, by, half, quarter)
        here = shard_refs[k].at[rows_of(k, half, quarter), :] if own else there
        return pltpu.make_async_remote_copy(
            src_ref=here,
            dst_ref=there,
            send_sem=send.at[k, bz],
            recv_sem=recv.at[k, bz],
            device_id=target,
            device_id_type=mesh_type,
        )

    def go_up(k, bz, own=False):
        return move(k, bz, y, group, None, up_sem, z_in, up, own)

    def go_down(k, bz, own=False):
        return move(k, bz, y, group, None, down_sem, z_in, down, own)

    def go_y(k, bz, by, own=False):
        return move(k, bz, by, group, None, y_sem, y_in, across, own)

    def go_x(k, bz, half):
        return move(k, bz, y, half, None, x_sem, x_in, other)

    def go_yq(k, bz, by, half, own=False):
        return move(k, bz, by, half, 1, yq_sem, yq_in, across, own)

    def go_xq(k, bz, half):
        return move(k, bz, 1 - y, half, 0, xq_sem, xq_in, other)

    def keep(k):
        wide = shard_refs[k].shape[1]
        start = pl.multiple_of(place * wide, 128)
        return pltpu.make_async_copy(
            shard_refs[k], out_refs[k].at[:, pl.ds(start, wide)], local_sem.at[k]
        )

    for k in range(count):

        @pl.when(has_up)
        def _(k=k):
            go_up(k, z, True).start()

        @pl.when(has_down)
        def _(k=k):
            go_down(k, z, True).start()

        go_y(k, z, y, True).start()
        go_yq(k, z, y, 1 - group, True).start()
        keep(k).start()

    for k in range(count):
        for step in range(1, Z_CHIPS):

            @pl.when(z - step >= 0)
            def _(k=k, step=step):
                block = z - step
                go_up(k, block).wait_recv()

                @pl.when(has_up)
                def _():
                    go_up(k, block).start()

                go_x(k, block, group).start()
                go_y(k, block, y).start()

            @pl.when(z + step < Z_CHIPS)
            def _(k=k, step=step):
                block = z + step
                go_down(k, block).wait_recv()

                @pl.when(has_down)
                def _():
                    go_down(k, block).start()

                go_x(k, block, group).start()
                go_y(k, block, y).start()

    for k in range(count):
        for block in range(Z_CHIPS):
            go_y(k, block, 1 - y).wait_recv()
            go_xq(k, block, group).start()

            @pl.when(z != block)
            def _(k=k, block=block):
                go_x(k, block, 1 - group).wait_recv()
                go_yq(k, block, y, 1 - group).start()

    for k in range(count):
        keep(k).wait()
        for block in range(Z_CHIPS):
            go_xq(k, block, 1 - group).wait_recv()
            go_yq(k, block, 1 - y, 1 - group).wait_recv()
            go_xq(k, block, group).wait_send()
            go_yq(k, block, y, 1 - group).wait_send()
            go_y(k, block, y).wait_send()

            @pl.when(z != block)
            def _(k=k, block=block):
                go_x(k, block, group).wait_send()

            @pl.when(jnp.logical_and(has_up, block <= z))
            def _(k=k, block=block):
                go_up(k, block).wait_send()

            @pl.when(jnp.logical_and(has_down, block >= z))
            def _(k=k, block=block):
                go_down(k, block).wait_send()


def gather_columns(*shards_in):
    count, ranks = len(shards_in), lax.axis_size("expert")
    fits = all(a.shape[1] % 128 == 0 and a.shape[0] % 64 == 0 for a in shards_in)
    if ranks != Z_CHIPS * Y_CHIPS or lax.axis_size("groups") != 2 or not fits:
        return [lax.all_gather(a, "expert", axis=1, tiled=True) for a in shards_in]
    return pl.pallas_call(
        lambda *refs: gather_kernel(count, *refs),
        out_shape=[
            jax.ShapeDtypeStruct((a.shape[0], a.shape[1] * ranks), a.dtype) for a in shards_in
        ],
        in_specs=[pl.BlockSpec(memory_space=pl.ANY)] * count,
        out_specs=[pl.BlockSpec(memory_space=pl.ANY)] * count,
        scratch_shapes=[pltpu.SemaphoreType.DMA((count,))]
        + [pltpu.SemaphoreType.DMA((count, Z_CHIPS))] * 11,
        compiler_params=pltpu.CompilerParams(collective_id=0, has_side_effects=True),
    )(*shards_in)


def halving_sum(rows):
    ranks, place = lax.axis_size("expert"), lax.axis_index("expert")
    if ranks & (ranks - 1):
        return lax.psum_scatter(rows, "expert", scatter_dimension=0, tiled=True)
    count = ranks.bit_length() - 1
    bits = list(range(count))[::-1]
    rows = rows.reshape((2,) * count + (rows.shape[0] // ranks, rows.shape[1]))
    for bit in [0] + bits[:-1]:
        axis, mine = bits.index(bit), (place >> bit) & 1
        bits.remove(bit)
        kept = lax.dynamic_index_in_dim(rows, mine, axis, keepdims=False)
        sent = lax.dynamic_index_in_dim(rows, 1 - mine, axis, keepdims=False)
        pairs = [(i, i ^ (1 << bit)) for i in range(ranks)]
        came = lax.ppermute(sent, "expert", pairs)
        rows = (kept.astype(jnp.float32) + came.astype(jnp.float32)).astype(jnp.bfloat16)
    return rows


def shards(
    stream,
    query_heads,
    key_heads,
    value_heads,
    out_proj,
    down_proj,
    expert_in,
    expert_out,
    up_proj,
    expert_ids,
    route_weights,
):
    length = stream.shape[0]
    out_full, down_full, up_full = gather_columns(out_proj, down_proj, up_proj)
    heads_out = attend(query_heads, key_heads, value_heads)
    rank_count = lax.axis_size("expert")
    local_experts = expert_in.shape[0]
    expert_count = local_experts * rank_count
    route_scale = route_weights.astype(jnp.float32) / 4096.0
    chosen = expert_ids[:, :, None] == jnp.arange(expert_count, dtype=jnp.int32)[None, None, :]
    gates = jnp.sum(jnp.where(chosen, route_scale[:, :, None], 0.0), axis=1)
    gates = lax.all_gather(gates, "expert", axis=0, tiled=True)
    gates = lax.dynamic_slice_in_dim(
        gates, lax.axis_index("expert") * local_experts, local_experts, axis=1
    )
    heads_out, gates = lax.optimization_barrier((heads_out, gates))
    attention = jnp.dot(
        heads_out,
        out_full,
        preferred_element_type=jnp.float32,
    )
    attention = lax.psum_scatter(attention, "tensor", scatter_dimension=1, tiled=True)
    hidden = (stream.astype(jnp.float32) + attention).astype(jnp.bfloat16)
    latent_part = jnp.dot(
        hidden,
        down_full,
        preferred_element_type=jnp.float32,
    )
    latent = lax.psum_scatter(latent_part, "tensor", scatter_dimension=0, tiled=True)
    latent = lax.all_gather(
        latent.astype(jnp.bfloat16), ("expert", "tensor"), axis=0, tiled=True
    )
    weight_out = expert_out.reshape(-1, expert_out.shape[2])
    totals = []
    for start in range(0, latent.shape[0], ROWS):
        rows = latent[start : start + ROWS]
        parts = []
        for e in range(local_experts):
            pre_act = jnp.dot(rows, expert_in[e], preferred_element_type=jnp.float32)
            gate = gates[start : start + ROWS, e : e + 1]
            parts.append((jnp.square(jnp.maximum(pre_act, 0.0)) * gate).astype(jnp.bfloat16))
        squared = jnp.concatenate(parts, axis=1)
        totals.append(
            jnp.dot(
                squared, weight_out, preferred_element_type=jnp.float32
            ).astype(jnp.bfloat16)
        )
    total = jnp.concatenate(totals, axis=0)
    combined = lax.psum_scatter(total, "tensor", scatter_dimension=1, tiled=True)
    combined = halving_sum(combined)
    lifted = jnp.dot(
        combined,
        up_full,
        preferred_element_type=jnp.float32,
    )
    lifted = lax.psum_scatter(lifted, "tensor", scatter_dimension=1, tiled=True)
    return (hidden.astype(jnp.float32) + lifted).astype(jnp.bfloat16)


def solution(mesh):
    return jax.shard_map(
        shards,
        mesh=mesh,
        in_specs=(
            P(("groups", "expert"), "tensor"),
            P(("groups", "expert"), "tensor"),
            P(("groups", "expert"), "tensor"),
            P(("groups", "expert"), "tensor"),
            P("tensor", "expert"),
            P("tensor", "expert"),
            P("expert", None, "tensor"),
            P("expert", "tensor", None),
            P("tensor", "expert"),
            P(("groups", "expert"), None),
            P(("groups", "expert"), None),
        ),
        out_specs=P(("groups", "expert"), "tensor"),
        check_vma=False,
    )
```
